32 devices in a mesh: src: 4 (over y, x), space: 8 (over z, core).
Axes of the slice: x: 2, y: 2, z: 4, core: 2. Of those that a mesh axis runs over, the one named last changes fastest.
Arguments:
- vectors: bfloat16 [3, 2, 9216, 128], P(None, None, 'space', 'src'), may hold values from -0.0625 to 0.0625
- lambdas: float32 [3, 128], replicated, may hold values from 0.01 to 0.2
- sources: bfloat16 [2, 9216, 512], P(None, 'space', 'src'), may hold values from -6 to 6
Outputs:
- propagated: bfloat16 [2, 9216, 512], P(None, 'space', 'src')
The draws below stay inside these ranges and needn't reach their ends.
All inputs are finite; a program needn't handle non-finite values.
Results may differ from the reference program's by a relative error of at most 0.0049.
Values may be sent and summed in bfloat16 or wider, within the bound.
No kernel may reach another device: no remote copies, remote signals or barrier semaphores. Data moves between devices by JAX's collectives and lax.ppermute only.
A program may use at most 64 MiB of HBM per device.

```python
import math
import jax
import jax.numpy as jnp

GROUP_MODES = 128
GROUPS = 3
ROWS = 9216
COLS = 512


def level_of(key, extent, pieces, smallest, high):
    def one(position, parts):
        draws = jax.random.uniform(jax.random.fold_in(jax.random.fold_in(key, 6), position), (parts,), jnp.float32, smallest / len(pieces), high / len(pieces))
        return jnp.repeat(jnp.exp(draws), extent[position] // parts).reshape((-1,) + (1,) * (len(extent) - position - 1))

    level = one(*pieces[0])
    for cut in pieces[1:]:
        level = level * one(*cut)
    return level


def bell_draw(key, shape, scale, reach, split=(), dtype=jnp.bfloat16):
    drawn = jax.random.normal(key, shape, jnp.float32) * scale
    if len(split) > 0:
        drawn = level_of(key, shape, split, -0.22, 0.18) * drawn
    return jnp.clip(drawn, min=-reach, max=reach).astype(dtype)


def setup_inputs(seed: int = 0) -> dict:
    splits = jax.random.split(jax.random.key(seed), 4)
    return {
        "vectors": bell_draw(splits[0], (GROUPS, 2, ROWS, GROUP_MODES), ROWS ** -0.5, 0.0625, ((2, 8), (3, 4))),
        "lambdas": jnp.clip(jnp.exp(jax.random.uniform(splits[1], (GROUPS, GROUP_MODES), jnp.float32, math.log(0.01), math.log(0.2))), 0.01, 0.2),
        "sources": bell_draw(splits[2], (2, ROWS, COLS), 1.0, 6.0, ((1, 8), (2, 4))),
    }


def reference(vectors, lambdas, sources):
    src_re = sources[0]
    src_im = sources[1]
    out_re = jnp.zeros((ROWS, COLS), jnp.float32)
    out_im = jnp.zeros((ROWS, COLS), jnp.float32)
    for number in range(GROUPS):
        vec_re = vectors[number, 0]
        vec_im = vectors[number, 1]
        coef_re = jnp.dot(vec_re.T, src_re, preferred_element_type=jnp.float32) + jnp.dot(vec_im.T, src_im, preferred_element_type=jnp.float32)
        coef_im = jnp.dot(vec_re.T, src_im, preferred_element_type=jnp.float32) - jnp.dot(vec_im.T, src_re, preferred_element_type=jnp.float32)
        factor = (1.0 / lambdas[number])[:, None]
        scaled_re = (coef_re * factor).astype(jnp.bfloat16)
        scaled_im = (coef_im * factor).astype(jnp.bfloat16)
        out_re = out_re + jnp.dot(vec_re, scaled_re, preferred_element_type=jnp.float32) - jnp.dot(vec_im, scaled_im, preferred_element_type=jnp.float32)
        out_im = out_im + jnp.dot(vec_re, scaled_im, preferred_element_type=jnp.float32) + jnp.dot(vec_im, scaled_re, preferred_element_type=jnp.float32)
    return jnp.stack([out_re, out_im]).astype(jnp.bfloat16)
```

```python
import functools

import jax
import jax.numpy as jnp
from jax import lax
from jax.experimental import pallas as pl
from jax.experimental.pallas import tpu as pltpu
from jax.sharding import PartitionSpec as P

VMEM = pl.BlockSpec(memory_space=pltpu.VMEM)
LIMIT = 40 * 1024 * 1024


def call(body, outs, args, flops=0):
    moved = sum(a.size * a.dtype.itemsize for a in list(args) + list(outs))
    return pl.pallas_call(
        body,
        out_shape=outs,
        in_specs=[VMEM] * len(args),
        out_specs=[VMEM] * len(outs),
        compiler_params=pltpu.CompilerParams(vmem_limit_bytes=LIMIT),
        cost_estimate=pl.CostEstimate(flops=flops, bytes_accessed=moved, transcendentals=0),
    )(*args)


def inverse_body(lam_ref, inv_ref):
    blocks, modes, cols = inv_ref.shape
    inverse = 1.0 / lam_ref[...]
    for k in range(blocks):
        inv_ref[k] = jnp.broadcast_to(inverse[k : k + 1, :], (cols, modes)).T


def project_body(count, *refs):
    pieces, (src_ref, mine_ref, theirs_ref) = refs[:count], refs[count:]
    keeps_real = lax.axis_index("space") % 2 == 0
    both = jnp.concatenate([src_ref[0], src_ref[1]], axis=1)
    cols = src_ref.shape[2]
    for i, piece in enumerate(pieces):
        blocks, _, modes, rows = piece.shape
        flat = piece[...].reshape(blocks * 2 * modes, rows)
        prod = jnp.dot(flat, both, preferred_element_type=jnp.float32)
        prod = prod.reshape(blocks, 2, modes, 2 * cols)
        real = prod[:, 0, :, :cols] + prod[:, 1, :, cols:]
        imag = prod[:, 0, :, cols:] - prod[:, 1, :, :cols]
        mine_ref[i] = jnp.where(keeps_real, real, imag)
        theirs_ref[i] = jnp.where(keeps_real, imag, real)


def add_body(*refs):
    total = refs[0][...]
    for ref in refs[1:-1]:
        total = total + ref[...]
    refs[-1][...] = total


def scale_body(places, per_device, *refs):
    parts, (inv_ref, out_ref) = refs[:-2], refs[-2:]
    me = lax.axis_index("src")
    _, blocks, modes, _ = out_ref.shape
    for i, (source, first) in enumerate(places):
        start = pl.multiple_of(source(me) * per_device + first, 8)
        total = parts[0][i]
        for part in parts[1:]:
            total = total + part[i]
        for k in range(blocks):
            factor = inv_ref[k, pl.ds(start, modes), :]
            out_ref[i, k] = (total[k] * factor).astype(out_ref.dtype)


def expand_body(counts, *refs):
    out_ref = refs[-1]
    keeps_real = lax.axis_index("space") % 2 == 0
    left, right, at = [], [], 0
    for count in counts:
        pieces, (mine_ref, theirs_ref) = refs[at : at + count], refs[at + count : at + count + 2]
        at += count + 2
        for i, piece in enumerate(pieces):
            blocks, _, modes, rows = piece.shape
            left.append(piece[...].reshape(blocks * 2 * modes, rows))
            mine, theirs = mine_ref[i], theirs_ref[i]
            real = jnp.where(keeps_real, mine, theirs)
            imag = jnp.where(keeps_real, theirs, mine)
            for k in range(blocks):
                right.append(jnp.concatenate([real[k], imag[k]], axis=1))
                right.append(jnp.concatenate([-imag[k], real[k]], axis=1))
    left = jnp.concatenate(left, axis=0)
    right = jnp.concatenate(right, axis=0)
    cols = out_ref.shape[2]
    out = lax.dot_general(left, right, (((0,), (0,)), ((), ())), preferred_element_type=jnp.float32)
    out_ref[0] = out[:, :cols].astype(out_ref.dtype)
    out_ref[1] = out[:, cols:].astype(out_ref.dtype)


def swap(x, axis, size, bit):
    return lax.ppermute(x, axis, [(i, i ^ bit) for i in range(size)])


def gather_pieces(own, n_src):
    modes = own.shape[2]
    if n_src == 4:
        half = modes // 2
        low, high = own[:, :, :half], own[:, :, half:]
        x = functools.partial(swap, axis="src", size=4, bit=1)
        y = functools.partial(swap, axis="src", size=4, bit=2)
        x_low, y_high = x(low), y(high)
        x_high, y_low = x(high), y(low)
        d_low, d_high = y(x_low), x(y_high)
        at = lambda q: lambda me: me ^ q
        return [
            [(low, at(0), 0), (high, at(0), half), (x_low, at(1), 0), (y_high, at(2), half)],
            [(x_high, at(1), half), (y_low, at(2), 0), (d_low, at(3), 0), (d_high, at(3), half)],
        ]
    group = [(own, lambda me: me, 0)]
    for step in range(1, n_src):
        piece = lax.ppermute(own, "src", [(i, (i + step) % n_src) for i in range(n_src)])
        group.append((piece, lambda me, step=step: (me + n_src - step) % n_src, 0))
    return [group]


def reduce_group(group, sources, inv, per_device, n_space):
    pieces = [p for p, _, _ in group]
    places = [(source, first) for _, source, first in group]
    blocks, _, modes, rows = pieces[0].shape
    cols = sources.shape[2]
    shape = (len(pieces), blocks, modes, cols)
    part = jax.ShapeDtypeStruct(shape, jnp.float32)
    mine, theirs = call(
        functools.partial(project_body, len(pieces)),
        [part, part],
        pieces + [sources],
        flops=8 * len(pieces) * blocks * modes * rows * cols,
    )
    arrived = swap(theirs, "space", n_space, 1)
    (total,) = call(add_body, [part], [mine, arrived])
    if n_space == 8:
        parts = [total] + [swap(total, "space", n_space, bit) for bit in (2, 4, 6)]
    else:
        bit = 2
        while bit < n_space:
            parts = [total, swap(total, "space", n_space, bit)]
            bit *= 2
            if bit < n_space:
                (total,) = call(add_body, [part], parts)
    (scaled,) = call(
        functools.partial(scale_body, places, per_device),
        [jax.ShapeDtypeStruct(shape, jnp.bfloat16)],
        parts + [inv],
    )
    return pieces, scaled, swap(scaled, "space", n_space, 1)


def on_device(n_src, n_space, vectors, lambdas, sources):
    own = jnp.swapaxes(vectors, 2, 3)
    blocks, _, per_device, rows = own.shape
    cols = sources.shape[2]
    (inv,) = call(inverse_body, [jax.ShapeDtypeStruct(lambdas.shape + (cols,), jnp.float32)], [lambdas])
    counts, args = [], []
    for group in gather_pieces(own, n_src):
        pieces, mine, theirs = reduce_group(group, sources, inv, per_device, n_space)
        counts.append(len(pieces))
        args += pieces + [mine, theirs]
    (out,) = call(
        functools.partial(expand_body, counts),
        [jax.ShapeDtypeStruct(sources.shape, jnp.bfloat16)],
        args,
        flops=8 * blocks * per_device * n_src * rows * cols,
    )
    return out


def solution(mesh):
    sizes = dict(mesh.shape)
    placed = (P(None, None, "space", "src"), P(), P(None, "space", "src"))
    return jax.shard_map(
        functools.partial(on_device, sizes["src"], sizes["space"]),
        mesh=mesh,
        in_specs=placed,
        out_specs=P(None, "space", "src"),
        check_vma=False,
    )
```

```python
import functools

import jax
import jax.numpy as jnp
from jax import lax
from jax.experimental import pallas as pl
from jax.experimental.pallas import tpu as pltpu
from jax.sharding import PartitionSpec as P

F32, BF16 = jnp.float32, jnp.bfloat16
VMEM = pl.BlockSpec(memory_space=pltpu.VMEM)
ANY = pl.BlockSpec(memory_space=pl.ANY)
LIMIT = 40 * 1024 * 1024


def call(body, outs, args, flops=0, after=(), scratch=()):
    moved = sum(a.size * a.dtype.itemsize for a in list(args) + list(outs))
    given, total = len(args), len(args) + len(after)

    def kernel(*refs):
        body(*refs[:given], *refs[total:])

    return pl.pallas_call(
        kernel,
        out_shape=outs,
        in_specs=[VMEM] * given + [ANY] * len(after),
        out_specs=[VMEM] * len(outs),
        scratch_shapes=list(scratch),
        compiler_params=pltpu.CompilerParams(vmem_limit_bytes=LIMIT),
        cost_estimate=pl.CostEstimate(flops=flops, bytes_accessed=moved, transcendentals=0),
    )(*args, *after)


def factors_body(groups, per_device, lam_ref, *refs):
    outs, inv = refs[:-1], refs[-1]
    blocks, modes, cols = inv.shape
    inverse = 1.0 / lam_ref[...]
    for k in range(blocks):
        inv[k] = jnp.broadcast_to(inverse[k : k + 1, :], (cols, modes)).T
    me = lax.axis_index("src")
    for out, group in zip(outs, groups):
        at = 0
        for source, first, count in group:
            start = pl.multiple_of(source(me) * per_device + first, 8)
            for k in range(blocks):
                out[at : at + count] = inv[k, pl.ds(start, count), :]
                at += count


def project_body(count, *refs):
    pieces, (src_ref, mine_ref, theirs_ref) = refs[:count], refs[count:]
    keeps_real = lax.axis_index("space") % 2 == 0
    both = jnp.concatenate([src_ref[0], src_ref[1]], axis=1)
    cols, modes = src_ref.shape[2], pieces[0].shape[2]
    flat = jnp.concatenate([p[...].reshape(-1, p.shape[-1]) for p in pieces], axis=0)
    prod = jnp.dot(flat, both, preferred_element_type=F32).reshape(-1, 2, modes, 2 * cols)
    real = prod[:, 0, :, :cols] + prod[:, 1, :, cols:]
    imag = prod[:, 0, :, cols:] - prod[:, 1, :, :cols]
    mine_ref[...] = jnp.where(keeps_real, real, imag).reshape(mine_ref.shape)
    theirs_ref[...] = jnp.where(keeps_real, imag, real).reshape(theirs_ref.shape)


def sums_body(pairs, *refs):
    for j in range(pairs):
        refs[2 * pairs + j][...] = refs[2 * j][...] + refs[2 * j + 1][...]


def scale_body(one, two, factor, out):
    out[...] = ((one[...] + two[...]) * factor[...]).astype(out.dtype)


def expand_body(counts, first, last, *refs):
    out_ref = refs[-1]
    at = 0 if first else 1
    keeps_real = lax.axis_index("space") % 2 == 0
    left, right = [], []
    for count in counts:
        pieces, (mine_ref, theirs_ref) = refs[at : at + count], refs[at + count : at + count + 2]
        at += count + 2
        row = 0
        for piece in pieces:
            blocks, _, modes, rows = piece.shape
            left.append(piece[...].reshape(blocks * 2 * modes, rows))
            for _ in range(blocks):
                mine, theirs = mine_ref[row : row + modes], theirs_ref[row : row + modes]
                row += modes
                real = jnp.where(keeps_real, mine, theirs)
                imag = jnp.where(keeps_real, theirs, mine)
                right.append(jnp.concatenate([real, imag], axis=1))
                right.append(jnp.concatenate([-imag, real], axis=1))
    left = jnp.concatenate(left, axis=0)
    right = jnp.concatenate(right, axis=0)
    out = lax.dot_general(left, right, (((0,), (0,)), ((), ())), preferred_element_type=F32)
    if not first:
        out = refs[0][...] + out
    if last:
        cols = out_ref.shape[2]
        out_ref[0] = out[:, :cols].astype(out_ref.dtype)
        out_ref[1] = out[:, cols:].astype(out_ref.dtype)
    else:
        out_ref[...] = out


def swap(x, axis, size, bit):
    return lax.ppermute(x, axis, [(i, i ^ bit) for i in range(size)])


def sums(*pairs):
    flat = [v for pair in pairs for v in pair]
    return call(
        functools.partial(sums_body, len(pairs)), [jax.ShapeDtypeStruct(a.shape, F32) for a, _ in pairs], flat
    )


def project(group, sources, n_space, after=()):
    pieces = [piece for piece, _, _ in group]
    _, rows, cols = sources.shape
    height = sum(p.shape[0] * p.shape[2] for p in pieces)
    part = jax.ShapeDtypeStruct((height, cols), F32)
    mine, theirs = call(
        functools.partial(project_body, len(pieces)),
        [part, part],
        pieces + [sources],
        flops=8 * height * rows * cols,
        after=after,
    )
    return mine, swap(theirs, "space", n_space, 1)


def scale(one, two, factor, n_space):
    (mine,) = call(scale_body, [jax.ShapeDtypeStruct(factor.shape, BF16)], [one, two, factor])
    return mine, swap(mine, "space", n_space, 1)


def factors_of(groups, lambdas, per_device, cols):
    blocks = lambdas.shape[0]
    places = [[(source, first, piece.shape[2]) for piece, source, first in group] for group in groups]
    heights = [sum(blocks * count for _, _, count in group) for group in places]
    return call(
        functools.partial(factors_body, places, per_device),
        [jax.ShapeDtypeStruct((height, cols), F32) for height in heights],
        [lambdas],
        scratch=[pltpu.VMEM(lambdas.shape + (cols,), F32)],
    )


def expand(stages, rows, cols):
    acc = None
    for number, stage in enumerate(stages):
        args = [] if acc is None else [acc]
        for group, mine, theirs in stage:
            args += [piece for piece, _, _ in group] + [mine, theirs]
        last = number == len(stages) - 1
        shape = jax.ShapeDtypeStruct((2, rows, cols), BF16) if last else jax.ShapeDtypeStruct((rows, 2 * cols), F32)
        body = functools.partial(expand_body, [len(group) for group, _, _ in stage], acc is None, last)
        (acc,) = call(body, [shape], args, flops=8 * rows * cols * sum(m.shape[0] for _, m, _ in stage))
    return acc


def on_square(vectors, lambdas, sources):
    own = jnp.swapaxes(vectors, 2, 3)
    per_device = own.shape[2]
    _, rows, cols = sources.shape
    half = per_device // 2
    x = functools.partial(swap, axis="src", size=4, bit=1)
    y = functools.partial(swap, axis="src", size=4, bit=2)
    near = functools.partial(swap, axis="space", size=8, bit=2)
    far = functools.partial(swap, axis="space", size=8, bit=4)
    at = lambda bits: lambda me: me ^ bits

    low, high = own[:, :, :half], own[:, :, half:]
    x_low, y_high = x(low), y(high)
    x_high, y_low = x(high), y(low)
    d_low, d_high = y(x_low), x(y_high)
    groups = [
        [(low, at(0), 0), (high, at(0), half), (x_low, at(1), 0), (y_high, at(2), half)],
        [(x_high, at(1), half), (y_low, at(2), 0)],
        [(d_low, at(3), 0), (d_high, at(3), half)],
    ]
    factors = factors_of(groups, lambdas, per_device, cols)

    mine, theirs = project(groups[0], sources, 8)
    (chip0,) = sums((mine, theirs))
    near0 = near(chip0)
    mine, theirs = project(groups[1], sources, 8, after=[chip0])
    (chip1,) = sums((mine, theirs))
    near1 = near(chip1)
    (pair0,) = sums((chip0, near0))
    far0 = far(pair0)
    mine, theirs = project(groups[2], sources, 8, after=[chip1])
    chip2, pair1 = sums((mine, theirs), (chip1, near1))
    near2 = near(chip2)
    far1 = far(pair1)
    (pair2,) = sums((chip2, near2))
    far2 = far(pair2)

    scaled = [
        (group,) + scale(pair, other, factor, 8)
        for group, pair, other, factor in zip(groups, (pair0, pair1, pair2), (far0, far1, far2), factors)
    ]
    return expand([scaled[:2], scaled[2:]], rows, cols)


def on_device(n_src, n_space, vectors, lambdas, sources):
    own = jnp.swapaxes(vectors, 2, 3)
    _, rows, cols = sources.shape
    group = [(own, lambda me: me, 0)]
    for step in range(1, n_src):
        piece = lax.ppermute(own, "src", [(i, (i + step) % n_src) for i in range(n_src)])
        group.append((piece, lambda me, step=step: (me + n_src - step) % n_src, 0))
    (factor,) = factors_of([group], lambdas, own.shape[2], cols)
    mine, theirs = project(group, sources, n_space)
    bit = 2
    while bit < n_space:
        (mine,) = sums((mine, theirs))
        theirs = swap(mine, "space", n_space, bit)
        bit *= 2
    return expand([[(group,) + scale(mine, theirs, factor, n_space)]], rows, cols)


def solution(mesh):
    n_src, n_space = mesh.shape["src"], mesh.shape["space"]
    assert n_space & (n_space - 1) == 0
    square = n_src == 4 and n_space == 8
    return jax.shard_map(
        on_square if square else functools.partial(on_device, n_src, n_space),
        mesh=mesh,
        in_specs=(P(None, None, "space", "src"), P(), P(None, "space", "src")),
        out_specs=P(None, "space", "src"),
        check_vma=False,
    )
```

```python
import functools

import jax
import jax.numpy as jnp
from jax import lax
from jax.experimental import pallas as pl
from jax.experimental.pallas import tpu as pltpu
from jax.sharding import PartitionSpec as P

F32, BF16 = jnp.float32, jnp.bfloat16
VMEM = pl.BlockSpec(memory_space=pltpu.VMEM)
ANY = pl.BlockSpec(memory_space=pl.ANY)
LIMIT = 40 * 1024 * 1024


def call(body, outs, args, flops=0, after=(), scratch=()):
    moved = sum(a.size * a.dtype.itemsize for a in list(args) + list(outs))
    given, total = len(args), len(args) + len(after)

    def kernel(*refs):
        body(*refs[:given], *refs[total:])

    return pl.pallas_call(
        kernel,
        out_shape=outs,
        in_specs=[VMEM] * given + [ANY] * len(after),
        out_specs=[VMEM] * len(outs),
        scratch_shapes=list(scratch),
        compiler_params=pltpu.CompilerParams(vmem_limit_bytes=LIMIT),
        cost_estimate=pl.CostEstimate(flops=flops, bytes_accessed=moved, transcendentals=0),
    )(*args, *after)


def factors_body(groups, per_device, lam_ref, *refs):
    outs, inv = refs[:-1], refs[-1]
    blocks, modes, cols = inv.shape
    inverse = 1.0 / lam_ref[...]
    for k in range(blocks):
        inv[k] = jnp.broadcast_to(inverse[k : k + 1, :], (cols, modes)).T
    me = lax.axis_index("src")
    for out, group in zip(outs, groups):
        at = 0
        for source, first, count in group:
            start = pl.multiple_of(source(me) * per_device + first, 8)
            for k in range(blocks):
                out[at : at + count] = inv[k, pl.ds(start, count), :]
                at += count


def project_body(count, *refs):
    pieces, (src_ref, mine_ref, theirs_ref) = refs[:count], refs[count:]
    keeps_real = lax.axis_index("space") % 2 == 0
    both = jnp.concatenate([src_ref[0], src_ref[1]], axis=1)
    cols, modes = src_ref.shape[2], pieces[0].shape[2]
    flat = jnp.concatenate([p[...].reshape(-1, p.shape[-1]) for p in pieces], axis=0)
    prod = jnp.dot(flat, both, preferred_element_type=F32).reshape(-1, 2, modes, 2 * cols)
    real = prod[:, 0, :, :cols] + prod[:, 1, :, cols:]
    imag = prod[:, 0, :, cols:] - prod[:, 1, :, :cols]
    mine_ref[...] = jnp.where(keeps_real, real, imag).reshape(mine_ref.shape)
    theirs_ref[...] = jnp.where(keeps_real, imag, real).reshape(theirs_ref.shape)


def sums_body(pairs, *refs):
    for j in range(pairs):
        refs[2 * pairs + j][...] = refs[2 * j][...] + refs[2 * j + 1][...]


def scale_body(one, two, factor, out):
    out[...] = ((one[...] + two[...]) * factor[...]).astype(out.dtype)


def expand_body(counts, first, last, *refs):
    out_ref = refs[-1]
    at = 0 if first else 1
    keeps_real = lax.axis_index("space") % 2 == 0
    left, right = [], []
    for count in counts:
        pieces, (mine_ref, theirs_ref) = refs[at : at + count], refs[at + count : at + count + 2]
        at += count + 2
        row = 0
        for piece in pieces:
            blocks, _, modes, rows = piece.shape
            left.append(piece[...].reshape(blocks * 2 * modes, rows))
            for _ in range(blocks):
                mine, theirs = mine_ref[row : row + modes], theirs_ref[row : row + modes]
                row += modes
                real = jnp.where(keeps_real, mine, theirs)
                imag = jnp.where(keeps_real, theirs, mine)
                right.append(jnp.concatenate([real, imag], axis=1))
                right.append(jnp.concatenate([-imag, real], axis=1))
    left = jnp.concatenate(left, axis=0)
    right = jnp.concatenate(right, axis=0)
    out = lax.dot_general(left, right, (((0,), (0,)), ((), ())), preferred_element_type=F32)
    if not first:
        out = refs[0][...] + out
    if last:
        cols = out_ref.shape[2]
        out_ref[0] = out[:, :cols].astype(out_ref.dtype)
        out_ref[1] = out[:, cols:].astype(out_ref.dtype)
    else:
        out_ref[...] = out


def turn_body(*refs):
    flat = jnp.concatenate([p[...].reshape(-1, p.shape[-1]) for p in refs[:-1]], axis=0)
    refs[-1][...] = flat.T


def finish_body(shapes, chunk, acc, turned, mine_ref, theirs_ref, out, held, sems):
    keeps_real = lax.axis_index("space") % 2 == 0
    right, row = [], 0
    for blocks, modes in shapes:
        for _ in range(blocks):
            mine, theirs = mine_ref[row : row + modes], theirs_ref[row : row + modes]
            row += modes
            real = jnp.where(keeps_real, mine, theirs)
            imag = jnp.where(keeps_real, theirs, mine)
            right.append(jnp.concatenate([real, imag], axis=1))
            right.append(jnp.concatenate([-imag, real], axis=1))
    right = jnp.concatenate(right, axis=0)
    _, rows, cols = held.shape
    copies = []
    for number, first in enumerate(range(0, rows, chunk)):
        some = pl.ds(first, chunk)
        both = acc[some, :] + jnp.dot(turned[some, :], right, preferred_element_type=F32)
        for part in range(2):
            held[part, some, :] = both[:, part * cols : (part + 1) * cols].astype(held.dtype)
            copy = pltpu.make_async_copy(held.at[part, some], out.at[part, some], sems.at[2 * number + part])
            copy.start()
            copies.append(copy)
    for copy in copies:
        copy.wait()


def finish(acc, group, mine, theirs, turned):
    rows, cols = acc.shape[0], mine.shape[1]
    chunk = rows // 3 if rows % 48 == 0 else rows
    shapes = [(piece.shape[0], piece.shape[2]) for piece, _, _ in group]
    return pl.pallas_call(
        functools.partial(finish_body, shapes, chunk),
        out_shape=jax.ShapeDtypeStruct((2, rows, cols), BF16),
        in_specs=[VMEM] * 4,
        out_specs=ANY,
        scratch_shapes=[pltpu.VMEM((2, rows, cols), BF16), pltpu.SemaphoreType.DMA((2 * (rows // chunk),))],
        compiler_params=pltpu.CompilerParams(vmem_limit_bytes=LIMIT),
    )(acc, turned, mine, theirs)


def swap(x, axis, size, bit):
    return lax.ppermute(x, axis, [(i, i ^ bit) for i in range(size)])


def sums(*pairs):
    flat = [v for pair in pairs for v in pair]
    return call(
        functools.partial(sums_body, len(pairs)), [jax.ShapeDtypeStruct(a.shape, F32) for a, _ in pairs], flat
    )


def project(group, sources, n_space, after=()):
    pieces = [piece for piece, _, _ in group]
    _, rows, cols = sources.shape
    height = sum(p.shape[0] * p.shape[2] for p in pieces)
    part = jax.ShapeDtypeStruct((height, cols), F32)
    mine, theirs = call(
        functools.partial(project_body, len(pieces)),
        [part, part],
        pieces + [sources],
        flops=8 * height * rows * cols,
        after=after,
    )
    return mine, swap(theirs, "space", n_space, 1)


def scale(one, two, factor, n_space, after=()):
    (mine,) = call(scale_body, [jax.ShapeDtypeStruct(factor.shape, BF16)], [one, two, factor], after=after)
    return mine, swap(mine, "space", n_space, 1)


def factors_of(groups, lambdas, per_device, cols):
    blocks = lambdas.shape[0]
    places = [[(source, first, piece.shape[2]) for piece, source, first in group] for group in groups]
    heights = [sum(blocks * count for _, _, count in group) for group in places]
    return call(
        functools.partial(factors_body, places, per_device),
        [jax.ShapeDtypeStruct((height, cols), F32) for height in heights],
        [lambdas],
        scratch=[pltpu.VMEM(lambdas.shape + (cols,), F32)],
    )


def expand(stages, rows, cols, whole=True):
    acc = None
    for number, stage in enumerate(stages):
        args = [] if acc is None else [acc]
        for group, mine, theirs in stage:
            args += [piece for piece, _, _ in group] + [mine, theirs]
        last = whole and number == len(stages) - 1
        shape = jax.ShapeDtypeStruct((2, rows, cols), BF16) if last else jax.ShapeDtypeStruct((rows, 2 * cols), F32)
        body = functools.partial(expand_body, [len(group) for group, _, _ in stage], acc is None, last)
        (acc,) = call(body, [shape], args, flops=8 * rows * cols * sum(m.shape[0] for _, m, _ in stage))
    return acc


def on_square(vectors, lambdas, sources):
    own = jnp.swapaxes(vectors, 2, 3)
    per_device = own.shape[2]
    _, rows, cols = sources.shape
    half = per_device // 2
    x = functools.partial(swap, axis="src", size=4, bit=1)
    y = functools.partial(swap, axis="src", size=4, bit=2)
    near = functools.partial(swap, axis="space", size=8, bit=2)
    far = functools.partial(swap, axis="space", size=8, bit=4)
    at = lambda bits: lambda me: me ^ bits

    low, high = own[:, :, :half], own[:, :, half:]
    x_low, y_high = x(low), y(high)
    x_high, y_low = x(high), y(low)
    d_low, d_high = y(x_low), x(y_high)
    groups = [
        [(low, at(0), 0), (high, at(0), half), (x_low, at(1), 0), (y_high, at(2), half)],
        [(x_high, at(1), half), (y_low, at(2), 0)],
        [(d_low, at(3), 0), (d_high, at(3), half)],
    ]
    factors = factors_of(groups, lambdas, per_device, cols)

    mine, theirs = project(groups[0], sources, 8)
    (chip0,) = sums((mine, theirs))
    near0 = near(chip0)
    mine, theirs = project(groups[1], sources, 8)
    (chip1,) = sums((mine, theirs))
    near1 = near(chip1)
    (pair0,) = sums((chip0, near0))
    far0 = far(pair0)
    mine, theirs = project(groups[2], sources, 8)
    chip2, pair1 = sums((mine, theirs), (chip1, near1))
    near2 = near(chip2)
    far1 = far(pair1)
    (pair2,) = sums((chip2, near2))
    far2 = far(pair2)

    pieces = [piece for piece, _, _ in groups[2]]
    wide = 2 * factors[2].shape[0]
    (turned,) = call(turn_body, [jax.ShapeDtypeStruct((rows, wide), BF16)], pieces, after=[chip2])
    first = (groups[0],) + scale(pair0, far0, factors[0], 8, after=[turned])
    second = (groups[1],) + scale(pair1, far1, factors[1], 8)
    mine, theirs = scale(pair2, far2, factors[2], 8)
    acc = expand([[first, second]], rows, cols, whole=False)
    return finish(acc, groups[2], mine, theirs, turned)


def on_device(n_src, n_space, vectors, lambdas, sources):
    own = jnp.swapaxes(vectors, 2, 3)
    _, rows, cols = sources.shape
    group = [(own, lambda me: me, 0)]
    for step in range(1, n_src):
        piece = lax.ppermute(own, "src", [(i, (i + step) % n_src) for i in range(n_src)])
        group.append((piece, lambda me, step=step: (me + n_src - step) % n_src, 0))
    (factor,) = factors_of([group], lambdas, own.shape[2], cols)
    mine, theirs = project(group, sources, n_space)
    bit = 2
    while bit < n_space:
        (mine,) = sums((mine, theirs))
        theirs = swap(mine, "space", n_space, bit)
        bit *= 2
    return expand([[(group,) + scale(mine, theirs, factor, n_space)]], rows, cols)


def solution(mesh):
    n_src, n_space = mesh.shape["src"], mesh.shape["space"]
    assert n_space & (n_space - 1) == 0
    square = n_src == 4 and n_space == 8
    return jax.shard_map(
        on_square if square else functools.partial(on_device, n_src, n_space),
        mesh=mesh,
        in_specs=(P(None, None, "space", "src"), P(), P(None, "space", "src")),
        out_specs=P(None, "space", "src"),
        check_vma=False,
    )
```

```python
import functools

import jax
import jax.numpy as jnp
from jax import lax
from jax.experimental import pallas as pl
from jax.experimental.pallas import tpu as pltpu
from jax.sharding import PartitionSpec as P

F32, BF16 = jnp.float32, jnp.bfloat16
VMEM = pl.BlockSpec(memory_space=pltpu.VMEM)
ANY = pl.BlockSpec(memory_space=pl.ANY)
LIMIT = 40 * 1024 * 1024


def call(body, outs, args, flops=0, after=(), scratch=()):
    moved = sum(a.size * a.dtype.itemsize for a in list(args) + list(outs))
    given, total = len(args), len(args) + len(after)

    def kernel(*refs):
        body(*refs[:given], *refs[total:])

    return pl.pallas_call(
        kernel,
        out_shape=outs,
        in_specs=[VMEM] * given + [ANY] * len(after),
        out_specs=[VMEM] * len(outs),
        scratch_shapes=list(scratch),
        compiler_params=pltpu.CompilerParams(vmem_limit_bytes=LIMIT),
        cost_estimate=pl.CostEstimate(flops=flops, bytes_accessed=moved, transcendentals=0),
    )(*args, *after)


def factors_body(groups, per_device, lam_ref, *refs):
    outs, inv = refs[:-1], refs[-1]
    blocks, modes, cols = inv.shape
    inverse = 1.0 / lam_ref[...]
    for k in range(blocks):
        inv[k] = jnp.broadcast_to(inverse[k : k + 1, :], (cols, modes)).T
    me = lax.axis_index("src")
    for out, group in zip(outs, groups):
        at = 0
        for source, first, count in group:
            start = pl.multiple_of(source(me) * per_device + first, 8)
            for k in range(blocks):
                out[at : at + count] = inv[k, pl.ds(start, count), :]
                at += count


def project_body(count, *refs):
    pieces, (src_ref, mine_ref, theirs_ref) = refs[:count], refs[count:]
    keeps_real = lax.axis_index("space") % 2 == 0
    both = jnp.concatenate([src_ref[0], src_ref[1]], axis=1)
    cols, modes = src_ref.shape[2], pieces[0].shape[2]
    flat = jnp.concatenate([p[...].reshape(-1, p.shape[-1]) for p in pieces], axis=0)
    prod = jnp.dot(flat, both, preferred_element_type=F32).reshape(-1, 2, modes, 2 * cols)
    real = prod[:, 0, :, :cols] + prod[:, 1, :, cols:]
    imag = prod[:, 0, :, cols:] - prod[:, 1, :, :cols]
    mine_ref[...] = jnp.where(keeps_real, real, imag).reshape(mine_ref.shape)
    theirs_ref[...] = jnp.where(keeps_real, imag, real).reshape(theirs_ref.shape)


def sums_body(pairs, *refs):
    for j in range(pairs):
        refs[2 * pairs + j][...] = refs[2 * j][...] + refs[2 * j + 1][...]


def scale_body(one, two, factor, out):
    out[...] = ((one[...] + two[...]) * factor[...]).astype(out.dtype)


def expand_body(counts, first, last, *refs):
    out_ref = refs[-1]
    at = 0 if first else 1
    keeps_real = lax.axis_index("space") % 2 == 0
    left, right = [], []
    for count in counts:
        pieces, (mine_ref, theirs_ref) = refs[at : at + count], refs[at + count : at + count + 2]
        at += count + 2
        row = 0
        for piece in pieces:
            blocks, _, modes, rows = piece.shape
            left.append(piece[...].reshape(blocks * 2 * modes, rows))
            for _ in range(blocks):
                mine, theirs = mine_ref[row : row + modes], theirs_ref[row : row + modes]
                row += modes
                real = jnp.where(keeps_real, mine, theirs)
                imag = jnp.where(keeps_real, theirs, mine)
                right.append(jnp.concatenate([real, imag], axis=1))
                right.append(jnp.concatenate([-imag, real], axis=1))
    left = jnp.concatenate(left, axis=0)
    right = jnp.concatenate(right, axis=0)
    out = lax.dot_general(left, right, (((0,), (0,)), ((), ())), preferred_element_type=F32)
    if not first:
        out = refs[0][...] + out
    if last:
        cols = out_ref.shape[2]
        out_ref[0] = out[:, :cols].astype(out_ref.dtype)
        out_ref[1] = out[:, cols:].astype(out_ref.dtype)
    else:
        out_ref[...] = out


def turn_body(*refs):
    flat = jnp.concatenate([p[...].reshape(-1, p.shape[-1]) for p in refs[:-1]], axis=0)
    refs[-1][...] = flat.T


def finish_body(shapes, chunk, acc, turned, mine_ref, theirs_ref, out, held, sems):
    keeps_real = lax.axis_index("space") % 2 == 0
    right, row = [], 0
    for blocks, modes in shapes:
        for _ in range(blocks):
            mine, theirs = mine_ref[row : row + modes], theirs_ref[row : row + modes]
            row += modes
            real = jnp.where(keeps_real, mine, theirs)
            imag = jnp.where(keeps_real, theirs, mine)
            right.append(jnp.concatenate([real, imag], axis=1))
            right.append(jnp.concatenate([-imag, real], axis=1))
    right = jnp.concatenate(right, axis=0)
    _, rows, cols = held.shape
    copies = []
    for number, first in enumerate(range(0, rows, chunk)):
        some = pl.ds(first, chunk)
        both = acc[some, :] + jnp.dot(turned[some, :], right, preferred_element_type=F32)
        for part in range(2):
            held[part, some, :] = both[:, part * cols : (part + 1) * cols].astype(held.dtype)
            copy = pltpu.make_async_copy(held.at[part, some], out.at[part, some], sems.at[2 * number + part])
            copy.start()
            copies.append(copy)
    for copy in copies:
        copy.wait()


def finish(acc, group, mine, theirs, turned):
    rows, cols = acc.shape[0], mine.shape[1]
    chunk = rows // 3 if rows % 48 == 0 else rows
    shapes = [(piece.shape[0], piece.shape[2]) for piece, _, _ in group]
    return pl.pallas_call(
        functools.partial(finish_body, shapes, chunk),
        out_shape=jax.ShapeDtypeStruct((2, rows, cols), BF16),
        in_specs=[VMEM] * 4,
        out_specs=ANY,
        scratch_shapes=[pltpu.VMEM((2, rows, cols), BF16), pltpu.SemaphoreType.DMA((2 * (rows // chunk),))],
        compiler_params=pltpu.CompilerParams(vmem_limit_bytes=LIMIT),
    )(acc, turned, mine, theirs)


def swap(x, axis, size, bit):
    return lax.ppermute(x, axis, [(i, i ^ bit) for i in range(size)])


def sums(*pairs):
    flat = [v for pair in pairs for v in pair]
    return call(
        functools.partial(sums_body, len(pairs)), [jax.ShapeDtypeStruct(a.shape, F32) for a, _ in pairs], flat
    )


def project(group, sources, n_space, after=()):
    pieces = [piece for piece, _, _ in group]
    _, rows, cols = sources.shape
    height = sum(p.shape[0] * p.shape[2] for p in pieces)
    part = jax.ShapeDtypeStruct((height, cols), F32)
    mine, theirs = call(
        functools.partial(project_body, len(pieces)),
        [part, part],
        pieces + [sources],
        flops=8 * height * rows * cols,
        after=after,
    )
    return mine, swap(theirs, "space", n_space, 1)


def scale(one, two, factor, n_space, after=()):
    (mine,) = call(scale_body, [jax.ShapeDtypeStruct(factor.shape, BF16)], [one, two, factor], after=after)
    return mine, swap(mine, "space", n_space, 1)


def factors_of(groups, lambdas, per_device, cols):
    blocks = lambdas.shape[0]
    places = [[(source, first, piece.shape[2]) for piece, source, first in group] for group in groups]
    heights = [sum(blocks * count for _, _, count in group) for group in places]
    return call(
        functools.partial(factors_body, places, per_device),
        [jax.ShapeDtypeStruct((height, cols), F32) for height in heights],
        [lambdas],
        scratch=[pltpu.VMEM(lambdas.shape + (cols,), F32)],
    )


def expand(stages, rows, cols, whole=True):
    acc = None
    for number, stage in enumerate(stages):
        args = [] if acc is None else [acc]
        for group, mine, theirs in stage:
            args += [piece for piece, _, _ in group] + [mine, theirs]
        last = whole and number == len(stages) - 1
        shape = jax.ShapeDtypeStruct((2, rows, cols), BF16) if last else jax.ShapeDtypeStruct((rows, 2 * cols), F32)
        body = functools.partial(expand_body, [len(group) for group, _, _ in stage], acc is None, last)
        (acc,) = call(body, [shape], args, flops=8 * rows * cols * sum(m.shape[0] for _, m, _ in stage))
    return acc


def on_square(vectors, lambdas, sources):
    own = jnp.swapaxes(vectors, 2, 3)
    per_device = own.shape[2]
    _, rows, cols = sources.shape
    half = per_device // 2
    x = functools.partial(swap, axis="src", size=4, bit=1)
    y = functools.partial(swap, axis="src", size=4, bit=2)
    near = functools.partial(swap, axis="space", size=8, bit=2)
    far = functools.partial(swap, axis="space", size=8, bit=4)
    at = lambda bits: lambda me: me ^ bits

    low, high = own[:, :, :half], own[:, :, half:]
    x_low, y_high = x(low), y(high)
    x_high, y_low = x(high), y(low)
    d_low, d_high = y(x_low), x(y_high)
    groups = [
        [(low, at(0), 0), (high, at(0), half), (x_low, at(1), 0), (y_high, at(2), half)],
        [(x_high, at(1), half), (y_low, at(2), 0)],
        [(d_low, at(3), 0), (d_high, at(3), half)],
    ]
    factors = factors_of(groups, lambdas, per_device, cols)

    mine, theirs = project(groups[0], sources, 8)
    (chip0,) = sums((mine, theirs))
    near0 = near(chip0)
    mine, theirs = project(groups[1], sources, 8)
    (chip1,) = sums((mine, theirs))
    near1 = near(chip1)
    (pair0,) = sums((chip0, near0))
    far0 = far(pair0)
    mine, theirs = project(groups[2], sources, 8)
    chip2, pair1 = sums((mine, theirs), (chip1, near1))
    near2 = near(chip2)
    far1 = far(pair1)
    (pair2,) = sums((chip2, near2))
    far2 = far(pair2)

    pieces = [piece for piece, _, _ in groups[2]]
    wide = 2 * factors[2].shape[0]
    (turned,) = call(turn_body, [jax.ShapeDtypeStruct((rows, wide), BF16)], pieces, after=[chip2])
    first = (groups[0],) + scale(pair0, far0, factors[0], 8, after=[turned])
    second = (groups[1],) + scale(pair1, far1, factors[1], 8)
    mine, theirs = scale(pair2, far2, factors[2], 8)
    acc = expand([[first], [second]], rows, cols, whole=False)
    return finish(acc, groups[2], mine, theirs, turned)


def on_device(n_src, n_space, vectors, lambdas, sources):
    own = jnp.swapaxes(vectors, 2, 3)
    _, rows, cols = sources.shape
    group = [(own, lambda me: me, 0)]
    for step in range(1, n_src):
        piece = lax.ppermute(own, "src", [(i, (i + step) % n_src) for i in range(n_src)])
        group.append((piece, lambda me, step=step: (me + n_src - step) % n_src, 0))
    (factor,) = factors_of([group], lambdas, own.shape[2], cols)
    mine, theirs = project(group, sources, n_space)
    bit = 2
    while bit < n_space:
        (mine,) = sums((mine, theirs))
        theirs = swap(mine, "space", n_space, bit)
        bit *= 2
    return expand([[(group,) + scale(mine, theirs, factor, n_space)]], rows, cols)


def solution(mesh):
    n_src, n_space = mesh.shape["src"], mesh.shape["space"]
    assert n_space & (n_space - 1) == 0
    square = n_src == 4 and n_space == 8
    return jax.shard_map(
        on_square if square else functools.partial(on_device, n_src, n_space),
        mesh=mesh,
        in_specs=(P(None, None, "space", "src"), P(), P(None, "space", "src")),
        out_specs=P(None, "space", "src"),
        check_vma=False,
    )
```

```python
import functools

import jax
import jax.numpy as jnp
from jax import lax
from jax.experimental import pallas as pl
from jax.experimental.pallas import tpu as pltpu
from jax.sharding import PartitionSpec as P

F32, BF16 = jnp.float32, jnp.bfloat16
VMEM = pl.BlockSpec(memory_space=pltpu.VMEM)
ANY = pl.BlockSpec(memory_space=pl.ANY)
LIMIT = 40 * 1024 * 1024


def call(body, outs, args, flops=0, after=(), scratch=()):
    moved = sum(a.size * a.dtype.itemsize for a in list(args) + list(outs))
    given, total = len(args), len(args) + len(after)

    def kernel(*refs):
        body(*refs[:given], *refs[total:])

    return pl.pallas_call(
        kernel,
        out_shape=outs,
        in_specs=[VMEM] * given + [ANY] * len(after),
        out_specs=[VMEM] * len(outs),
        scratch_shapes=list(scratch),
        compiler_params=pltpu.CompilerParams(vmem_limit_bytes=LIMIT),
        cost_estimate=pl.CostEstimate(flops=flops, bytes_accessed=moved, transcendentals=0),
    )(*args, *after)


def factors_body(groups, per_device, lam_ref, *refs):
    outs, inv = refs[:-1], refs[-1]
    blocks, modes, cols = inv.shape
    inverse = 1.0 / lam_ref[...]
    for k in range(blocks):
        inv[k] = jnp.broadcast_to(inverse[k : k + 1, :], (cols, modes)).T
    me = lax.axis_index("src")
    for out, group in zip(outs, groups):
        at = 0
        for source, first, count in group:
            start = pl.multiple_of(source(me) * per_device + first, 8)
            for k in range(blocks):
                out[at : at + count] = inv[k, pl.ds(start, count), :]
                at += count


def project_body(count, *refs):
    pieces, (src_ref, mine_ref, theirs_ref) = refs[:count], refs[count:]
    keeps_real = lax.axis_index("space") % 2 == 0
    both = jnp.concatenate([src_ref[0], src_ref[1]], axis=1)
    cols, modes = src_ref.shape[2], pieces[0].shape[2]
    flat = jnp.concatenate([p[...].reshape(-1, p.shape[-1]) for p in pieces], axis=0)
    prod = jnp.dot(flat, both, preferred_element_type=F32).reshape(-1, 2, modes, 2 * cols)
    real = prod[:, 0, :, :cols] + prod[:, 1, :, cols:]
    imag = prod[:, 0, :, cols:] - prod[:, 1, :, :cols]
    mine_ref[...] = jnp.where(keeps_real, real, imag).reshape(mine_ref.shape)
    theirs_ref[...] = jnp.where(keeps_real, imag, real).reshape(theirs_ref.shape)


def sums_body(pairs, *refs):
    for j in range(pairs):
        refs[2 * pairs + j][...] = refs[2 * j][...] + refs[2 * j + 1][...]


def scale_body(one, two, factor, out):
    out[...] = ((one[...] + two[...]) * factor[...]).astype(out.dtype)


def expand_body(counts, first, last, *refs):
    out_ref = refs[-1]
    at = 0 if first else 1
    keeps_real = lax.axis_index("space") % 2 == 0
    left, right = [], []
    for count in counts:
        pieces, (mine_ref, theirs_ref) = refs[at : at + count], refs[at + count : at + count + 2]
        at += count + 2
        row = 0
        for piece in pieces:
            blocks, _, modes, rows = piece.shape
            left.append(piece[...].reshape(blocks * 2 * modes, rows))
            for _ in range(blocks):
                mine, theirs = mine_ref[row : row + modes], theirs_ref[row : row + modes]
                row += modes
                real = jnp.where(keeps_real, mine, theirs)
                imag = jnp.where(keeps_real, theirs, mine)
                right.append(jnp.concatenate([real, imag], axis=1))
                right.append(jnp.concatenate([-imag, real], axis=1))
    left = jnp.concatenate(left, axis=0)
    right = jnp.concatenate(right, axis=0)
    out = lax.dot_general(left, right, (((0,), (0,)), ((), ())), preferred_element_type=F32)
    if not first:
        out = refs[0][...] + out
    if last:
        cols = out_ref.shape[2]
        out_ref[0] = out[:, :cols].astype(out_ref.dtype)
        out_ref[1] = out[:, cols:].astype(out_ref.dtype)
    else:
        out_ref[...] = out


def turn_body(*refs):
    flat = jnp.concatenate([p[...].reshape(-1, p.shape[-1]) for p in refs[:-1]], axis=0)
    refs[-1][...] = flat.T


def finish_body(shapes, chunk, acc, turned, mine_ref, theirs_ref, out, held, sems):
    keeps_real = lax.axis_index("space") % 2 == 0
    right, row = [], 0
    for blocks, modes in shapes:
        for _ in range(blocks):
            mine, theirs = mine_ref[row : row + modes], theirs_ref[row : row + modes]
            row += modes
            real = jnp.where(keeps_real, mine, theirs)
            imag = jnp.where(keeps_real, theirs, mine)
            right.append(jnp.concatenate([real, imag], axis=1))
            right.append(jnp.concatenate([-imag, real], axis=1))
    right = jnp.concatenate(right, axis=0)
    _, rows, cols = held.shape
    copies = []
    for number, first in enumerate(range(0, rows, chunk)):
        some = pl.ds(first, chunk)
        both = acc[some, :] + jnp.dot(turned[some, :], right, preferred_element_type=F32)
        for part in range(2):
            held[part, some, :] = both[:, part * cols : (part + 1) * cols].astype(held.dtype)
            copy = pltpu.make_async_copy(held.at[part, some], out.at[part, some], sems.at[2 * number + part])
            copy.start()
            copies.append(copy)
    for copy in copies:
        copy.wait()


def finish(acc, group, mine, theirs, turned):
    rows, cols = acc.shape[0], mine.shape[1]
    chunk = rows // 3 if rows % 48 == 0 else rows
    shapes = [(piece.shape[0], piece.shape[2]) for piece, _, _ in group]
    return pl.pallas_call(
        functools.partial(finish_body, shapes, chunk),
        out_shape=jax.ShapeDtypeStruct((2, rows, cols), BF16),
        in_specs=[VMEM] * 4,
        out_specs=ANY,
        scratch_shapes=[pltpu.VMEM((2, rows, cols), BF16), pltpu.SemaphoreType.DMA((2 * (rows // chunk),))],
        compiler_params=pltpu.CompilerParams(vmem_limit_bytes=LIMIT),
    )(acc, turned, mine, theirs)


def swap(x, axis, size, bit):
    return lax.ppermute(x, axis, [(i, i ^ bit) for i in range(size)])


def sums(*pairs):
    flat = [v for pair in pairs for v in pair]
    return call(
        functools.partial(sums_body, len(pairs)), [jax.ShapeDtypeStruct(a.shape, F32) for a, _ in pairs], flat
    )


def project(group, sources, n_space, after=()):
    pieces = [piece for piece, _, _ in group]
    _, rows, cols = sources.shape
    height = sum(p.shape[0] * p.shape[2] for p in pieces)
    part = jax.ShapeDtypeStruct((height, cols), F32)
    mine, theirs = call(
        functools.partial(project_body, len(pieces)),
        [part, part],
        pieces + [sources],
        flops=8 * height * rows * cols,
        after=after,
    )
    return mine, swap(theirs, "space", n_space, 1)


def scale(one, two, factor, n_space, after=()):
    (mine,) = call(scale_body, [jax.ShapeDtypeStruct(factor.shape, BF16)], [one, two, factor], after=after)
    return mine, swap(mine, "space", n_space, 1)


def factors_of(groups, lambdas, per_device, cols):
    blocks = lambdas.shape[0]
    places = [[(source, first, piece.shape[2]) for piece, source, first in group] for group in groups]
    heights = [sum(blocks * count for _, _, count in group) for group in places]
    return call(
        functools.partial(factors_body, places, per_device),
        [jax.ShapeDtypeStruct((height, cols), F32) for height in heights],
        [lambdas],
        scratch=[pltpu.VMEM(lambdas.shape + (cols,), F32)],
    )


def expand(stages, rows, cols, whole=True):
    acc = None
    for number, stage in enumerate(stages):
        args = [] if acc is None else [acc]
        for group, mine, theirs in stage:
            args += [piece for piece, _, _ in group] + [mine, theirs]
        last = whole and number == len(stages) - 1
        shape = jax.ShapeDtypeStruct((2, rows, cols), BF16) if last else jax.ShapeDtypeStruct((rows, 2 * cols), F32)
        body = functools.partial(expand_body, [len(group) for group, _, _ in stage], acc is None, last)
        (acc,) = call(body, [shape], args, flops=8 * rows * cols * sum(m.shape[0] for _, m, _ in stage))
    return acc


def on_square(vectors, lambdas, sources):
    own = jnp.swapaxes(vectors, 2, 3)
    per_device = own.shape[2]
    _, rows, cols = sources.shape
    half = per_device // 2
    x = functools.partial(swap, axis="src", size=4, bit=1)
    y = functools.partial(swap, axis="src", size=4, bit=2)
    near = functools.partial(swap, axis="space", size=8, bit=2)
    far = functools.partial(swap, axis="space", size=8, bit=4)
    at = lambda bits: lambda me: me ^ bits

    low, high = own[:, :, :half], own[:, :, half:]
    x_low, y_high = x(low), y(high)
    x_high, y_low = x(high), y(low)
    d_low, d_high = y(x_low), x(y_high)
    groups = [
        [(low, at(0), 0), (high, at(0), half), (x_low, at(1), 0), (y_high, at(2), half)],
        [(x_high, at(1), half), (y_low, at(2), 0)],
        [(d_low, at(3), 0), (d_high, at(3), half)],
    ]
    factors = factors_of(groups, lambdas, per_device, cols)

    mine, theirs = project(groups[0], sources, 8)
    (chip0,) = sums((mine, theirs))
    near0 = near(chip0)
    mine, theirs = project(groups[1], sources, 8)
    (chip1,) = sums((mine, theirs))
    near1 = near(chip1)
    (pair0,) = sums((chip0, near0))
    far0 = far(pair0)
    mine, theirs = project(groups[2], sources, 8)
    chip2, pair1 = sums((mine, theirs), (chip1, near1))
    near2 = near(chip2)
    far1 = far(pair1)
    (pair2,) = sums((chip2, near2))
    far2 = far(pair2)

    pieces = [piece for piece, _, _ in groups[2]]
    wide = 2 * factors[2].shape[0]
    (turned,) = call(turn_body, [jax.ShapeDtypeStruct((rows, wide), BF16)], pieces, after=[pair2])
    first = (groups[0],) + scale(pair0, far0, factors[0], 8, after=[turned])
    second = (groups[1],) + scale(pair1, far1, factors[1], 8)
    mine, theirs = scale(pair2, far2, factors[2], 8)
    acc = expand([[first, second]], rows, cols, whole=False)
    return finish(acc, groups[2], mine, theirs, turned)


def on_device(n_src, n_space, vectors, lambdas, sources):
    own = jnp.swapaxes(vectors, 2, 3)
    _, rows, cols = sources.shape
    group = [(own, lambda me: me, 0)]
    for step in range(1, n_src):
        piece = lax.ppermute(own, "src", [(i, (i + step) % n_src) for i in range(n_src)])
        group.append((piece, lambda me, step=step: (me + n_src - step) % n_src, 0))
    (factor,) = factors_of([group], lambdas, own.shape[2], cols)
    mine, theirs = project(group, sources, n_space)
    bit = 2
    while bit < n_space:
        (mine,) = sums((mine, theirs))
        theirs = swap(mine, "space", n_space, bit)
        bit *= 2
    return expand([[(group,) + scale(mine, theirs, factor, n_space)]], rows, cols)


def solution(mesh):
    n_src, n_space = mesh.shape["src"], mesh.shape["space"]
    assert n_space & (n_space - 1) == 0
    square = n_src == 4 and n_space == 8
    return jax.shard_map(
        on_square if square else functools.partial(on_device, n_src, n_space),
        mesh=mesh,
        in_specs=(P(None, None, "space", "src"), P(), P(None, "space", "src")),
        out_specs=P(None, "space", "src"),
        check_vma=False,
    )
```

```python
import functools

import jax
import jax.numpy as jnp
from jax import lax
from jax.experimental import pallas as pl
from jax.experimental.pallas import tpu as pltpu
from jax.sharding import PartitionSpec as P

F32, BF16 = jnp.float32, jnp.bfloat16
VMEM = pl.BlockSpec(memory_space=pltpu.VMEM)
ANY = pl.BlockSpec(memory_space=pl.ANY)
LIMIT = 40 * 1024 * 1024


def call(body, outs, args, flops=0, after=(), scratch=()):
    moved = sum(a.size * a.dtype.itemsize for a in list(args) + list(outs))
    given, total = len(args), len(args) + len(after)

    def kernel(*refs):
        body(*refs[:given], *refs[total:])

    return pl.pallas_call(
        kernel,
        out_shape=outs,
        in_specs=[VMEM] * given + [ANY] * len(after),
        out_specs=[VMEM] * len(outs),
        scratch_shapes=list(scratch),
        compiler_params=pltpu.CompilerParams(vmem_limit_bytes=LIMIT),
        cost_estimate=pl.CostEstimate(flops=flops, bytes_accessed=moved, transcendentals=0),
    )(*args, *after)


def factors_body(groups, per_device, lam_ref, *refs):
    outs, inv = refs[:-1], refs[-1]
    blocks, modes, cols = inv.shape
    inverse = 1.0 / lam_ref[...]
    for k in range(blocks):
        inv[k] = jnp.broadcast_to(inverse[k : k + 1, :], (cols, modes)).T
    me = lax.axis_index("src")
    for out, group in zip(outs, groups):
        at = 0
        for source, first, count in group:
            start = pl.multiple_of(source(me) * per_device + first, 8)
            for k in range(blocks):
                out[at : at + count] = inv[k, pl.ds(start, count), :]
                at += count


def project_body(count, *refs):
    pieces, (src_ref, mine_ref, theirs_ref) = refs[:count], refs[count:]
    keeps_real = lax.axis_index("space") % 2 == 0
    both = jnp.concatenate([src_ref[0], src_ref[1]], axis=1)
    cols, modes = src_ref.shape[2], pieces[0].shape[2]
    flat = jnp.concatenate([p[...].reshape(-1, p.shape[-1]) for p in pieces], axis=0)
    prod = jnp.dot(flat, both, preferred_element_type=F32).reshape(-1, 2, modes, 2 * cols)
    real = prod[:, 0, :, :cols] + prod[:, 1, :, cols:]
    imag = prod[:, 0, :, cols:] - prod[:, 1, :, :cols]
    mine_ref[...] = jnp.where(keeps_real, real, imag).reshape(mine_ref.shape)
    theirs_ref[...] = jnp.where(keeps_real, imag, real).reshape(theirs_ref.shape)


def sums_body(pairs, *refs):
    for j in range(pairs):
        refs[2 * pairs + j][...] = refs[2 * j][...] + refs[2 * j + 1][...]


def scale_body(one, two, factor, out):
    out[...] = ((one[...] + two[...]) * factor[...]).astype(out.dtype)


def expand_body(counts, first, last, *refs):
    out_ref = refs[-1]
    at = 0 if first else 1
    keeps_real = lax.axis_index("space") % 2 == 0
    left, right = [], []
    for count in counts:
        pieces, (mine_ref, theirs_ref) = refs[at : at + count], refs[at + count : at + count + 2]
        at += count + 2
        row = 0
        for piece in pieces:
            blocks, _, modes, rows = piece.shape
            left.append(piece[...].reshape(blocks * 2 * modes, rows))
            for _ in range(blocks):
                mine, theirs = mine_ref[row : row + modes], theirs_ref[row : row + modes]
                row += modes
                real = jnp.where(keeps_real, mine, theirs)
                imag = jnp.where(keeps_real, theirs, mine)
                right.append(jnp.concatenate([real, imag], axis=1))
                right.append(jnp.concatenate([-imag, real], axis=1))
    left = jnp.concatenate(left, axis=0)
    right = jnp.concatenate(right, axis=0)
    out = lax.dot_general(left, right, (((0,), (0,)), ((), ())), preferred_element_type=F32)
    if not first:
        out = refs[0][...] + out
    if last:
        cols = out_ref.shape[2]
        out_ref[0] = out[:, :cols].astype(out_ref.dtype)
        out_ref[1] = out[:, cols:].astype(out_ref.dtype)
    else:
        out_ref[...] = out


def turn_body(*refs):
    flat = jnp.concatenate([p[...].reshape(-1, p.shape[-1]) for p in refs[:-1]], axis=0)
    refs[-1][...] = flat.T


def finish_body(shapes, chunk, acc, turned, mine_ref, theirs_ref, out, held, sems):
    keeps_real = lax.axis_index("space") % 2 == 0
    right, row = [], 0
    for blocks, modes in shapes:
        for _ in range(blocks):
            mine, theirs = mine_ref[row : row + modes], theirs_ref[row : row + modes]
            row += modes
            real = jnp.where(keeps_real, mine, theirs)
            imag = jnp.where(keeps_real, theirs, mine)
            right.append(jnp.concatenate([real, imag], axis=1))
            right.append(jnp.concatenate([-imag, real], axis=1))
    right = jnp.concatenate(right, axis=0)
    _, rows, cols = held.shape
    copies = []
    for number, first in enumerate(range(0, rows, chunk)):
        some = pl.ds(first, chunk)
        both = acc[some, :] + jnp.dot(turned[some, :], right, preferred_element_type=F32)
        for part in range(2):
            held[part, some, :] = both[:, part * cols : (part + 1) * cols].astype(held.dtype)
            copy = pltpu.make_async_copy(held.at[part, some], out.at[part, some], sems.at[2 * number + part])
            copy.start()
            copies.append(copy)
    for copy in copies:
        copy.wait()


def finish(acc, group, mine, theirs, turned):
    rows, cols = acc.shape[0], mine.shape[1]
    chunk = rows // 2 if rows % 32 == 0 else rows
    shapes = [(piece.shape[0], piece.shape[2]) for piece, _, _ in group]
    return pl.pallas_call(
        functools.partial(finish_body, shapes, chunk),
        out_shape=jax.ShapeDtypeStruct((2, rows, cols), BF16),
        in_specs=[VMEM] * 4,
        out_specs=ANY,
        scratch_shapes=[pltpu.VMEM((2, rows, cols), BF16), pltpu.SemaphoreType.DMA((2 * (rows // chunk),))],
        compiler_params=pltpu.CompilerParams(vmem_limit_bytes=LIMIT),
    )(acc, turned, mine, theirs)


def swap(x, axis, size, bit):
    return lax.ppermute(x, axis, [(i, i ^ bit) for i in range(size)])


def sums(*pairs):
    flat = [v for pair in pairs for v in pair]
    return call(
        functools.partial(sums_body, len(pairs)), [jax.ShapeDtypeStruct(a.shape, F32) for a, _ in pairs], flat
    )


def project(group, sources, n_space, after=()):
    pieces = [piece for piece, _, _ in group]
    _, rows, cols = sources.shape
    height = sum(p.shape[0] * p.shape[2] for p in pieces)
    part = jax.ShapeDtypeStruct((height, cols), F32)
    mine, theirs = call(
        functools.partial(project_body, len(pieces)),
        [part, part],
        pieces + [sources],
        flops=8 * height * rows * cols,
        after=after,
    )
    return mine, swap(theirs, "space", n_space, 1)


def scale(one, two, factor, n_space, after=()):
    (mine,) = call(scale_body, [jax.ShapeDtypeStruct(factor.shape, BF16)], [one, two, factor], after=after)
    return mine, swap(mine, "space", n_space, 1)


def factors_of(groups, lambdas, per_device, cols):
    blocks = lambdas.shape[0]
    places = [[(source, first, piece.shape[2]) for piece, source, first in group] for group in groups]
    heights = [sum(blocks * count for _, _, count in group) for group in places]
    return call(
        functools.partial(factors_body, places, per_device),
        [jax.ShapeDtypeStruct((height, cols), F32) for height in heights],
        [lambdas],
        scratch=[pltpu.VMEM(lambdas.shape + (cols,), F32)],
    )


def expand(stages, rows, cols, whole=True):
    acc = None
    for number, stage in enumerate(stages):
        args = [] if acc is None else [acc]
        for group, mine, theirs in stage:
            args += [piece for piece, _, _ in group] + [mine, theirs]
        last = whole and number == len(stages) - 1
        shape = jax.ShapeDtypeStruct((2, rows, cols), BF16) if last else jax.ShapeDtypeStruct((rows, 2 * cols), F32)
        body = functools.partial(expand_body, [len(group) for group, _, _ in stage], acc is None, last)
        (acc,) = call(body, [shape], args, flops=8 * rows * cols * sum(m.shape[0] for _, m, _ in stage))
    return acc


def on_square(vectors, lambdas, sources):
    own = jnp.swapaxes(vectors, 2, 3)
    per_device = own.shape[2]
    _, rows, cols = sources.shape
    half = per_device // 2
    x = functools.partial(swap, axis="src", size=4, bit=1)
    y = functools.partial(swap, axis="src", size=4, bit=2)
    near = functools.partial(swap, axis="space", size=8, bit=2)
    far = functools.partial(swap, axis="space", size=8, bit=4)
    at = lambda bits: lambda me: me ^ bits

    low, high = own[:, :, :half], own[:, :, half:]
    x_low, y_high = x(low), y(high)
    x_high, y_low = x(high), y(low)
    d_low, d_high = y(x_low), x(y_high)
    groups = [
        [(low, at(0), 0), (high, at(0), half), (x_low, at(1), 0), (y_high, at(2), half)],
        [(x_high, at(1), half), (y_low, at(2), 0)],
        [(d_low, at(3), 0), (d_high, at(3), half)],
    ]
    factors = factors_of(groups, lambdas, per_device, cols)

    mine, theirs = project(groups[0], sources, 8)
    (chip0,) = sums((mine, theirs))
    near0 = near(chip0)
    mine, theirs = project(groups[1], sources, 8)
    (chip1,) = sums((mine, theirs))
    near1 = near(chip1)
    (pair0,) = sums((chip0, near0))
    far0 = far(pair0)
    mine, theirs = project(groups[2], sources, 8)
    chip2, pair1 = sums((mine, theirs), (chip1, near1))
    near2 = near(chip2)
    far1 = far(pair1)
    (pair2,) = sums((chip2, near2))
    far2 = far(pair2)

    pieces = [piece for piece, _, _ in groups[2]]
    wide = 2 * factors[2].shape[0]
    (turned,) = call(turn_body, [jax.ShapeDtypeStruct((rows, wide), BF16)], pieces, after=[chip2])
    first = (groups[0],) + scale(pair0, far0, factors[0], 8, after=[turned])
    second = (groups[1],) + scale(pair1, far1, factors[1], 8)
    mine, theirs = scale(pair2, far2, factors[2], 8)
    acc = expand([[first, second]], rows, cols, whole=False)
    return finish(acc, groups[2], mine, theirs, turned)


def on_device(n_src, n_space, vectors, lambdas, sources):
    own = jnp.swapaxes(vectors, 2, 3)
    _, rows, cols = sources.shape
    group = [(own, lambda me: me, 0)]
    for step in range(1, n_src):
        piece = lax.ppermute(own, "src", [(i, (i + step) % n_src) for i in range(n_src)])
        group.append((piece, lambda me, step=step: (me + n_src - step) % n_src, 0))
    (factor,) = factors_of([group], lambdas, own.shape[2], cols)
    mine, theirs = project(group, sources, n_space)
    bit = 2
    while bit < n_space:
        (mine,) = sums((mine, theirs))
        theirs = swap(mine, "space", n_space, bit)
        bit *= 2
    return expand([[(group,) + scale(mine, theirs, factor, n_space)]], rows, cols)


def solution(mesh):
    n_src, n_space = mesh.shape["src"], mesh.shape["space"]
    assert n_space & (n_space - 1) == 0
    square = n_src == 4 and n_space == 8
    return jax.shard_map(
        on_square if square else functools.partial(on_device, n_src, n_space),
        mesh=mesh,
        in_specs=(P(None, None, "space", "src"), P(), P(None, "space", "src")),
        out_specs=P(None, "space", "src"),
        check_vma=False,
    )
```
